32 devices in a mesh: dp: 4 (over y, core), tm: 8 (over z, x).
Axes of the slice: x: 2, y: 2, z: 4, core: 2. Of those that a mesh axis runs over, the one named last changes fastest.
Arguments:
- frames: bfloat16 [8192, 1536], P(('dp', 'tm')), may hold values from -28 to 28, as said below
- seg: int32 [4, 2048], P('dp'), may hold values from 0 to 3, never falling along the last dimension, each value on 1 to 1024 neighbouring positions
- look_back: int32 [4, 8], P('dp'), may hold values 0 or 1
- w_dw: float32 [5, 1536], replicated, may hold values from -2.5 to 2.5
- w_qkv: bfloat16 [1536, 4608], P(None, 'dp'), may hold values from -0.15625 to 0.15625
- w_o: bfloat16 [1536, 1536], replicated, may hold values from -1.5 to 1.5
- cotangent: bfloat16 [8192, 1536], P(('dp', 'tm')), may hold values from -0.23925781 to 0.23925781
Outputs:
- mixed: bfloat16 [8192, 1536], P(('dp', 'tm'))
- weight_grad: float32 [1536, 1536], P('tm', 'dp')
The draws below stay inside these ranges and needn't reach their ends.
Inputs may be any that keep to these rules, and one draw needn't show every extreme that they name: Float features; a few short runs of frames may be several times larger than the rest. `seg`: recording numbers never fall along a replica's frames; each recording has 1 to 1024 frames, one exactly 1024.
All inputs are finite; a program needn't handle non-finite values. No bound on the sum of `look_back` on one device may be relied on, other than what follows from the above.
Results may differ from the reference program's by a relative error of at most 0.012.
The reference program's roundings to bfloat16 on the way count: a program that leaves them out, or rounds other values in their place, can miss the bound.
Values may be sent and summed in bfloat16 or wider, within the bound.
No kernel may reach another device: no remote copies, remote signals or barrier semaphores. Data moves between devices by JAX's collectives and lax.ppermute only.
A program may use at most 128 MiB of HBM per device.

```python
import math
import jax
import jax.numpy as jnp
import numpy as np
from jax import lax

D = 1536
HEADS = 16
KER = 5
HDIM = 96
STRETCH = 256
REC = 4
FR = 2048
FRAMES = 8192
NCH = 8
MOST = 1024
N_DP = 4


def draw_frames(key, part):
    first_key = jax.random.fold_in(key, 0)
    values = jnp.clip(jax.random.normal(first_key, (FRAMES, D), jnp.float32), -6.0, 6.0)
    return values.astype(jnp.bfloat16)


def plant(values, key, smallest, largest):
    dims = values.shape
    index_at = [jax.random.randint(jax.random.fold_in(key, axis), (), 0, dims[axis]) for axis in range(len(dims))]
    values = values.at[tuple(index_at)].set(smallest)
    longest = dims.index(max(dims))
    index_at[longest] = (index_at[longest] + 1) % dims[longest]
    return values.at[tuple(index_at)].set(largest)


def spiked(values, own_key, source, target, blocks, factor):
    owner, partner = [(jnp.arange(values.shape[dim]) // (values.shape[dim] // blocks)).reshape([-1 if axis == dim else 1 for axis in range(values.ndim)]) for dim in (source, target)]
    chosen = jax.random.permutation(own_key, blocks)[partner]
    strong = (owner == chosen) | (owner == (partner + blocks // 2) % blocks)
    return jnp.where(strong, factor * values, values)


def steps_of(rng, dims, pieces, smallest, top_value):
    gain, own = 1.0, jax.random.fold_in(rng, 6)
    for axis_at, shards_of in pieces:
        draws = jnp.exp(jax.random.uniform(jax.random.fold_in(own, axis_at), (shards_of,), jnp.float32, smallest / len(pieces), top_value / len(pieces)))
        gain = gain * jnp.repeat(draws, dims[axis_at] // shards_of).reshape([-1 if axis == axis_at else 1 for axis in range(len(dims))])
    return gain


def length_profile(count, total, bound, lean):
    loads = [(1 << 20) // math.isqrt(grade ** lean) + 1 for grade in range(2, count + 1)]
    spare, holding = total - bound - (count - 1), [1] * (count - 1)
    while spare > 0:
        movable = [i for i in range(count - 1) if holding[i] < bound]
        pool, remaining = sum([loads[i] for i in movable]), spare
        for i in movable:
            addition = min(bound - holding[i], max(1, remaining * loads[i] // pool), spare)
            holding[i] = holding[i] + addition
            spare = spare - addition
    return np.array([bound] + holding)


def ragged_sizes(rng, count, total, bound, skew):
    if count == 2:
        one = jax.random.randint(rng, (), max(1, total - bound), min(bound, total - 1) + 1)
        return jnp.stack([one, total - one])
    sizes = jnp.asarray(length_profile(count, total, bound, skew), jnp.int32)
    twos = (count - 1) // 2
    giver, sink = sizes[1:1 + 2 * twos:2], sizes[2:2 + 2 * twos:2]
    margin = jnp.minimum(giver - 1, bound - sink)
    shifted = jax.random.randint(jax.random.fold_in(rng, 1), (twos,), 0, 1 << 20) % (margin + 1)
    sizes = sizes.at[1:1 + 2 * twos:2].set(giver - shifted).at[2:2 + 2 * twos:2].set(sink + shifted)
    return sizes[jax.random.permutation(jax.random.fold_in(rng, 2), count)]


def bell_draw(own_key, shape, scale, bound, cuts=(), kind=jnp.bfloat16):
    values = jax.random.normal(own_key, shape, jnp.float32) * scale
    if len(cuts) > 0:
        values = steps_of(own_key, shape, cuts, -0.22, 0.18) * values
    return jnp.clip(values, min=-bound, max=bound).astype(kind)


def heavy_noise(own_key, extent, deviation, limit, cuts, heavy, held_as=jnp.bfloat16):
    drawn = deviation * jax.random.normal(own_key, extent, jnp.float32)
    if cuts:
        drawn = drawn * steps_of(own_key, extent, cuts, -0.22, 0.18)
    return jnp.clip(spiked(drawn, jax.random.fold_in(own_key, 3), *heavy), -limit, limit).astype(held_as)


def setup_inputs(seed: int = 0) -> dict:
    arg_keys = jax.random.split(jax.random.key(seed), 8)
    frames = draw_frames(jax.random.fold_in(arg_keys[7], 71), 0)
    seg = jax.vmap(lambda own: jnp.searchsorted(jnp.cumsum(ragged_sizes(own, REC, FR, MOST, 1)), jnp.arange(FR), side="right"))(jax.random.split(arg_keys[1], N_DP)).reshape((N_DP, FR)).astype(jnp.int32)
    look_back = plant((jax.random.randint(arg_keys[2], (N_DP, NCH), 0, 4) < 3).astype(jnp.int32), jax.random.fold_in(arg_keys[2], 1), 0, 1)
    w_dw = bell_draw(arg_keys[3], (KER, D), KER ** -0.5, 2.5, (), jnp.float32)
    w_qkv = bell_draw(arg_keys[4], (D, 3 * D), D ** -0.5, 0.15625, ((1, 4),))
    w_o = bell_draw(arg_keys[5], (D, D), 16 ** -0.5, 1.5)
    cotangent = heavy_noise(arg_keys[6], (FRAMES, D), 0.04, 0.23925781, ((0, 32),), (0, 1, 32, 2.75))
    return dict(frames=frames, seg=seg, look_back=look_back, w_dw=w_dw, w_qkv=w_qkv, w_o=w_o, cotangent=cotangent)


def stretch_attention(queries, keys, values, seg_row, look_row, stretch):
    frame_count, heads_here, head_dim = queries.shape
    value_dim = values.shape[2]
    blocks = frame_count // stretch
    query_blocks = queries.reshape(blocks, stretch, heads_here, head_dim)
    key_blocks = keys.reshape(blocks, stretch, heads_here, head_dim)
    value_blocks = values.reshape(blocks, stretch, heads_here, value_dim)
    key_pairs = jnp.concatenate([jnp.concatenate([jnp.zeros_like(key_blocks[:1]), key_blocks[:-1]], 0), key_blocks], 1)
    value_pairs = jnp.concatenate([jnp.concatenate([jnp.zeros_like(value_blocks[:1]), value_blocks[:-1]], 0), value_blocks], 1)
    seg_blocks = seg_row.reshape(blocks, stretch)
    seg_pairs = jnp.concatenate([jnp.concatenate([jnp.full((1, stretch), -1, jnp.int32), seg_blocks[:-1]], 0), seg_blocks], 1)
    allow_prev = look_row == 1
    per_step = math.gcd(blocks, max(1, 512 // stretch))
    current = jnp.arange(2 * stretch) >= stretch
    scale = 1.0 / math.sqrt(head_dim)

    def block_step(block_index):
        start = (block_index * per_step).astype(jnp.int32)

        def pick_rows(array):
            return lax.dynamic_slice_in_dim(array, start, per_step, 0)
        scores = jnp.einsum('gqhd,gkhd->ghqk', pick_rows(query_blocks).astype(jnp.float32), pick_rows(key_pairs).astype(jnp.float32)) * scale
        same_rec = pick_rows(seg_pairs)[:, None, :] == pick_rows(seg_blocks)[:, :, None]
        allowed = same_rec & (current[None, None, :] | pick_rows(allow_prev)[:, None, None])
        scores = jnp.where(allowed[:, None], scores, -1e+30)
        row_max = lax.optimization_barrier(jnp.max(scores, axis=-1, keepdims=True))
        raw_weights = jnp.exp(scores - row_max)
        probs = (raw_weights / lax.optimization_barrier(jnp.sum(raw_weights, axis=-1, keepdims=True))).astype(jnp.bfloat16)
        outputs = jnp.einsum('ghqk,gkhv->gqhv', probs.astype(jnp.float32), pick_rows(value_pairs).astype(jnp.float32))
        return outputs.astype(jnp.bfloat16).reshape(per_step * stretch, heads_here * value_dim)
    mixed = lax.map(block_step, jnp.arange(blocks // per_step, dtype=jnp.int32))
    return mixed.reshape(frame_count, heads_here * value_dim)

def conv_silu(frames_rep, seg_row, w_dw):
    count = frames_rep.shape[0]
    half = KER // 2
    padded = jnp.pad(frames_rep.astype(jnp.float32), ((half, half), (0, 0)))
    seg_padded = jnp.pad(seg_row, (half, half), constant_values=-1)
    total = jnp.zeros(frames_rep.shape, jnp.float32)
    for offset in range(KER):
        same_rec = (seg_padded[offset:offset + count] == seg_row).astype(jnp.float32)
        total = total + w_dw[offset] * padded[offset:offset + count] * same_rec[:, None]
    return jax.nn.silu(total).astype(jnp.bfloat16)

def replica_forward(frames_rep, seg_row, look_row, w_dw, w_qkv, w_o):
    activ = conv_silu(frames_rep, seg_row, w_dw)
    qkv = jnp.dot(activ, w_qkv, preferred_element_type=jnp.float32).astype(jnp.bfloat16)

    def head_step(head):
        first = (head * HDIM).astype(jnp.int32)
        queries = lax.dynamic_slice_in_dim(qkv, first, HDIM, 1)
        keys = lax.dynamic_slice_in_dim(qkv, first + D, HDIM, 1)
        values = lax.dynamic_slice_in_dim(qkv, first + 2 * D, HDIM, 1)
        return stretch_attention(queries[:, None, :], keys[:, None, :], values[:, None, :], seg_row, look_row, STRETCH)
    per_head = lax.map(head_step, jnp.arange(HEADS, dtype=jnp.int32))
    attn = per_head.transpose(1, 0, 2).reshape(FR, D)
    mixed = jnp.dot(attn, w_o, preferred_element_type=jnp.float32).astype(jnp.bfloat16)
    return (mixed, attn)

def reference(frames, seg, look_back, w_dw, w_qkv, w_o, cotangent):
    stacked = frames.reshape(N_DP, FR, D)

    def replica_step(items):
        return replica_forward(items[0], items[1], items[2], w_dw, w_qkv, w_o)
    mixed, attn = lax.map(replica_step, (stacked, seg, look_back))
    mixed = mixed.reshape(FRAMES, D)
    weight_grad = lax.dot_general(attn.reshape(FRAMES, D).astype(jnp.float32), cotangent.astype(jnp.float32), (((0,), (0,)), ((), ())))
    return (mixed, weight_grad)
```

```python
import math

import jax
import jax.numpy as jnp
from jax import lax
from jax.experimental import pallas as pl
from jax.experimental.pallas import tpu as pltpu
from jax.sharding import PartitionSpec as P

KER = 5
HDIM = 96
STRETCH = 256
GROUP = 4
COLS = GROUP * HDIM
EDGE = 16
MIB = 1 << 20
LITTLE = pl.CostEstimate(flops=10**6, bytes_accessed=10**4, transcendentals=0)

ORDERS = (
    ((0, 1, 2), (1, 2, 0), (2, 0, 1), (0, 1, 2)),
    ((2, 0, 1), (0, 1, 2), (0, 1, 2), (1, 2, 0)),
)
SENT_SLOT = [
    sum(ORDERS[f][d][r] << 2 * (4 * f + d) for f in range(2) for d in range(4)) for r in range(3)
]
SENT_ROUND = [
    sum(ORDERS[f][d].index(s) << 2 * (4 * f + d) for f in range(2) for d in range(4))
    for s in range(3)
]


def in_hbm(block):
    return pltpu.with_memory_space_constraint(block, pltpu.HBM)


def shifted(block, axis, step):
    count = lax.axis_size(axis)
    route = [(i, i + step) for i in range(count) if 0 <= i + step < count]
    return lax.ppermute(block, axis, route)


def crossed(block, axis, bits):
    count = lax.axis_size(axis)
    return lax.ppermute(block, axis, [(i, i ^ bits) for i in range(count)])


def after(block, *earlier):
    return lax.optimization_barrier((block, *earlier))[0]


def picked(packed, first, owner):
    return (packed >> (2 * (4 * first + owner))) & 3


def place_bits():
    at, place = lax.axis_index("tm"), lax.axis_index("dp")
    return at, place, 1 - at // 4, (at ^ (at >> 1)) & 1


def masks_kernel(look_ref, seg_ref, same_ref, bias_ref, segs):
    rows = bias_ref.shape[0]
    at = lax.axis_index("tm")
    half = KER // 2
    segs[...] = jnp.full(segs.shape, -1.0, jnp.float32)
    segs[:, rows + 128 : rows + 128 + seg_ref.shape[1]] = seg_ref[...].astype(jnp.float32)
    window = segs[:, pl.ds(pl.multiple_of(at * rows, 128), 2 * rows + 256)]
    mid = window[:, 128 : 128 + 2 * rows]
    lines = jnp.broadcast_to(mid, (128, 2 * rows))
    line = lax.broadcasted_iota(jnp.int32, (128, 2 * rows), 0)
    for o in range(KER):
        start = 128 + o - half
        equal = (window[:, start : start + 2 * rows] == mid).astype(jnp.float32)
        lines = jnp.where(line == o, jnp.broadcast_to(equal, lines.shape), lines)
    columns = lines.T
    same_ref[...] = columns
    col = lax.broadcasted_iota(jnp.int32, (rows, 2 * rows), 1)
    kept = (columns[rows:, KER : KER + 1] == mid) & ((col >= rows) | (look_ref[0, at] == 1))
    bias_ref[...] = jnp.where(kept, 0.0, -1e30)


def masks(look_back, seg, rows):
    vmem = pl.BlockSpec(memory_space=pltpu.VMEM)
    return pl.pallas_call(
        masks_kernel,
        out_shape=(
            jax.ShapeDtypeStruct((2 * rows, 128), jnp.float32),
            jax.ShapeDtypeStruct((rows, 2 * rows), jnp.float32),
        ),
        in_specs=[pl.BlockSpec(memory_space=pltpu.SMEM), vmem],
        out_specs=(vmem, vmem),
        scratch_shapes=[pltpu.VMEM((1, seg.shape[1] + 2 * rows + 256), jnp.float32)],
        compiler_params=pltpu.CompilerParams(vmem_limit_bytes=8 * MIB),
        cost_estimate=LITTLE,
        name="masks",
    )(look_back, seg)


def conv_kernel(far_ref, prev_ref, own_ref, next_ref, same_ref, taps_ref, act_ref, wide):
    rows = own_ref.shape[0]
    width = own_ref.shape[1]
    wide[0:EDGE] = far_ref[...].astype(jnp.float32)
    wide[EDGE : EDGE + rows] = prev_ref[...].astype(jnp.float32)
    wide[EDGE + rows : EDGE + 2 * rows] = own_ref[...].astype(jnp.float32)
    wide[EDGE + 2 * rows : 2 * EDGE + 2 * rows] = next_ref[...].astype(jnp.float32)
    part = 64
    half = KER // 2

    for start in range(0, 2 * rows, part):
        same = [
            jnp.broadcast_to(same_ref[start : start + part, o : o + 1], (part, 128))
            for o in range(KER)
        ]
        for col in range(0, width, 128):
            total = None
            for o in range(KER):
                first = EDGE + start + o - half
                term = (
                    taps_ref[o : o + 1, col : col + 128]
                    * wide[first : first + part, col : col + 128]
                )
                if o != half:
                    term = term * same[o]
                total = term if total is None else total + term
            total = 0.5 * total
            act_ref[start : start + part, col : col + 128] = (
                total + total * jnp.tanh(total)
            ).astype(jnp.bfloat16)


def conv_silu(far, prev, own, following, same, taps):
    rows, width = own.shape
    return pl.pallas_call(
        conv_kernel,
        out_shape=jax.ShapeDtypeStruct((2 * rows, width), jnp.bfloat16),
        scratch_shapes=[pltpu.VMEM((2 * EDGE + 2 * rows, width), jnp.float32)],
        compiler_params=pltpu.CompilerParams(vmem_limit_bytes=16 * MIB),
        cost_estimate=LITTLE,
        name="conv_silu",
    )(far, prev, own, following, same, taps)


def copies(pairs, sems):
    moves = [pltpu.make_async_copy(a, b, sems.at[i]) for i, (a, b) in enumerate(pairs)]
    for move in moves:
        move.start()
    for move in moves:
        move.wait()


def block_of(w_ref, turn):
    place, first, flip = place_bits()[1:]
    rows = w_ref.shape[0] // 2
    slot = picked(SENT_SLOT[turn], first, place)
    return w_ref.at[
        pl.ds(pl.multiple_of(flip * rows, rows), rows),
        pl.ds(pl.multiple_of(slot * COLS, 128), COLS),
    ]


def first_slice(w_ref, out_ref, sems):
    copies([(block_of(w_ref, turn), out_ref.at[turn]) for turn in range(2)], sems)


def later_slices(w_ref, cot_ref, _, *refs):
    place = lax.axis_index("dp")
    last, cot_own, cot_side, cot_two, sems = refs
    cots = (cot_own, cot_side, cot_two.at[0], cot_two.at[1])
    part = cot_ref.shape[1] // 4
    pairs = [(block_of(w_ref, 2), last)]
    for bits, ref in enumerate(cots):
        cols = pl.ds(pl.multiple_of((place ^ bits) * part, 128), part)
        pairs.append((cot_ref.at[:, cols], ref))
    copies(pairs, sems)


def sliced(kernel, name, out_shape, *blocks):
    anywhere = pl.BlockSpec(memory_space=pl.ANY)
    return pl.pallas_call(
        kernel,
        out_shape=out_shape,
        in_specs=[anywhere] * len(blocks),
        out_specs=[anywhere] * len(out_shape),
        scratch_shapes=[pltpu.SemaphoreType.DMA((8,))],
        compiler_params=pltpu.CompilerParams(vmem_limit_bytes=MIB),
        cost_estimate=LITTLE,
        name=name,
    )(*[in_hbm(block) for block in blocks[:2]], *blocks[2:])


def heads_kernel(sources, turn_in_order, act_ref, bias_ref, *refs):
    weight_refs, (own_ref, out_ref, held, sems) = refs[:-4], refs[-4:]
    rows = own_ref.shape[0]
    weight_refs, ahead_ref = weight_refs[:-1], weight_refs[-1]
    if ahead_ref is not None:
        out_ref[:, :COLS] = ahead_ref[...]
    width = act_ref.shape[1]
    half = width // 2
    scale = math.log2(math.e) / math.sqrt(HDIM)
    place, first, flip = place_bits()[1:]
    ring = len(sources) > 1
    if ring:
        group = 2 * (first ^ (turn_in_order // 2)) + turn_in_order % 2
    else:
        group, flip = turn_in_order, 0
    low_half = pl.ds(pl.multiple_of(flip * half, half), half)
    high_half = pl.ds(pl.multiple_of((1 - flip) * half, half), half)

    def fetch(kind):
        block = 4 * kind + group
        sem = sems.at[kind]
        target = held.at[kind]
        if ring:
            owner = (block * 11) >> 5
            slot = block - 3 * owner
            distance = owner ^ place
            code = jnp.where(
                slot == 0, SENT_ROUND[0], jnp.where(slot == 1, SENT_ROUND[1], SENT_ROUND[2])
            )
            sent_in = picked(code, first, owner)
        else:
            slot, distance = block, 0
        for form, which, refs_here in sources:
            wanted = distance == which
            if form == "first":
                wanted = wanted & (sent_in < 2)
            elif form == "last":
                wanted = wanted & (sent_in == 2)

            @pl.when(wanted)
            def _():
                if form == "whole":
                    ref = weight_refs[refs_here[0]]
                    cols = pl.ds(pl.multiple_of(slot * COLS, 128), COLS)
                    pltpu.make_async_copy(ref.at[low_half, cols], target.at[0:half], sem).start()
                    pltpu.make_async_copy(
                        ref.at[high_half, cols], target.at[half:width], sem
                    ).start()
                else:
                    start = 0
                    for index in refs_here:
                        ref = weight_refs[index]
                        if form == "first":
                            ref = ref.at[jnp.minimum(sent_in, 1)]
                        stop = start + ref.shape[0]
                        pltpu.make_async_copy(ref, target.at[start:stop], sem).start()
                        start = stop

    def project(kind, first_row):
        pltpu.make_async_copy(held.at[kind], held.at[kind], sems.at[kind]).wait()
        total = jnp.dot(
            act_ref[first_row:, low_half], held[kind, 0:half], preferred_element_type=jnp.float32
        ) + jnp.dot(
            act_ref[first_row:, high_half],
            held[kind, half:width],
            preferred_element_type=jnp.float32,
        )
        return total.astype(jnp.bfloat16)

    for kind in range(3):
        fetch(kind)
    queries = project(0, rows)
    keys = project(1, 0)
    values = project(2, 0)
    pieces = [None] * (COLS // 128)
    for head in range(GROUP):
        low, high = head * HDIM, (head + 1) * HDIM
        first_tile, last_tile = low // 128, -(-high // 128)
        window = slice(first_tile * 128, last_tile * 128)
        lanes = (rows, (last_tile - first_tile) * 128)
        lane = lax.broadcasted_iota(jnp.int32, lanes, 1) + first_tile * 128
        mine = (lane >= low) & (lane < high)
        one = jnp.where(mine, queries[:, window], jnp.zeros((), jnp.bfloat16))
        scores = lax.dot_general(
            one, keys[:, window], (((1,), (1,)), ((), ())), preferred_element_type=jnp.float32
        )
        scores = scores * scale + bias_ref[...]
        raw = jnp.exp2(scores - jnp.max(scores, axis=1, keepdims=True))
        mixed = jnp.dot(
            raw.astype(jnp.bfloat16), values[:, window], preferred_element_type=jnp.float32
        ) * (1.0 / jnp.sum(raw, axis=1, keepdims=True))
        for tile in range(first_tile, last_tile):
            here = slice((tile - first_tile) * 128, (tile - first_tile + 1) * 128)
            if pieces[tile] is None:
                pieces[tile] = mixed[:, here]
            else:
                pieces[tile] = jnp.where(mine[:, here], mixed[:, here], pieces[tile])
    for tile, piece in enumerate(pieces):
        block = piece.astype(jnp.bfloat16)
        own_ref[:, tile * 128 : (tile + 1) * 128] = block
        if ahead_ref is not None:
            out_ref[:, COLS + tile * 128 : COLS + (tile + 1) * 128] = block


def attend(sources, turn_in_order, weights, act, bias, *ahead):
    rows, width = act.shape[0] // 2, act.shape[1]
    vmem = pl.BlockSpec(memory_space=pltpu.VMEM)
    anywhere = pl.BlockSpec(memory_space=pl.ANY)

    def kernel(act_ref, bias_ref, *refs):
        if not ahead:
            refs = refs[:-3] + (None, refs[-3], None) + refs[-2:]
        heads_kernel(sources, turn_in_order, act_ref, bias_ref, *refs)

    outs = [jax.ShapeDtypeStruct((rows, COLS * n), jnp.bfloat16) for n in range(1, 2 + len(ahead))]
    return pl.pallas_call(
        kernel,
        out_shape=outs,
        in_specs=[vmem, vmem] + [anywhere] * len(weights) + [vmem] * len(ahead),
        out_specs=[vmem] * len(outs),
        scratch_shapes=[
            pltpu.VMEM((3, width, COLS), jnp.bfloat16),
            pltpu.SemaphoreType.DMA((3,)),
        ],
        compiler_params=pltpu.CompilerParams(vmem_limit_bytes=16 * MIB),
        cost_estimate=LITTLE,
        name=f"attention_{turn_in_order}",
    )(act, bias, in_hbm(weights[0]), *weights[1:], *ahead)


def mixed_kernel(far_ref, near_ref, w_ref, out_ref):
    depth = far_ref.shape[1]
    first = place_bits()[2]
    far_rows, near_rows = (
        pl.ds(pl.multiple_of(pair * depth, depth), depth) for pair in (first, 1 - first)
    )
    total = jnp.dot(
        far_ref[...], w_ref[far_rows], preferred_element_type=jnp.float32
    ) + jnp.dot(near_ref[...], w_ref[near_rows], preferred_element_type=jnp.float32)
    out_ref[...] = total.astype(jnp.bfloat16)


def project_out(attns, w_o):
    rows, width = attns[0].shape[0], w_o.shape[1]
    cols = 512
    return pl.pallas_call(
        mixed_kernel,
        grid=(width // cols,),
        out_shape=jax.ShapeDtypeStruct((rows, width), jnp.bfloat16),
        in_specs=[pl.BlockSpec(attn.shape, lambda i: (0, 0)) for attn in attns]
        + [pl.BlockSpec((width, cols), lambda i: (0, i))],
        out_specs=pl.BlockSpec((rows, cols), lambda i: (0, i)),
        compiler_params=pltpu.CompilerParams(
            dimension_semantics=("arbitrary",), vmem_limit_bytes=16 * MIB
        ),
        cost_estimate=LITTLE,
        name="mixed",
    )(*attns, in_hbm(w_o))


def product(attn, cot):
    return lax.dot_general(attn, cot, (((0,), (0,)), ((), ())), preferred_element_type=jnp.float32)


def grad_kernel(*refs):
    *attn_refs, cot_0, cot_1, cot_2, cot_3, keep_ref, send_1, send_2, send_3, total = refs
    size = keep_ref.shape[0]
    low = lax.axis_index("tm") & 3
    for half in range(2):
        cols = slice(half * COLS, (half + 1) * COLS)
        blocks = [ref[:, cols] for ref in attn_refs if ref.shape[1] > COLS]
        blocks += [ref[...] for ref in attn_refs[len(blocks) + half :: 2]]
        cots = (cot_0[...], cot_1[...], cot_2[0], cot_3[1])
        total[cols] = sum(product(block, cot) for block, cot in zip(blocks, cots))
    keep_ref[...] = total[pl.ds(pl.multiple_of(low * size, size), size)]
    for bits, ref in enumerate((send_1, send_2, send_3), 1):
        ref[...] = total[pl.ds(pl.multiple_of((low ^ bits) * size, size), size)].astype(
            jnp.bfloat16
        )


def grad_part(attns, cots, name):
    cols = cots[0].shape[1]
    size = COLS // 2
    return pl.pallas_call(
        grad_kernel,
        out_shape=[jax.ShapeDtypeStruct((size, cols), jnp.float32)]
        + [jax.ShapeDtypeStruct((size, cols), jnp.bfloat16)] * 3,
        scratch_shapes=[pltpu.VMEM((2 * COLS, cols), jnp.float32)],
        compiler_params=pltpu.CompilerParams(vmem_limit_bytes=16 * MIB),
        cost_estimate=LITTLE,
        name=name,
    )(*attns, *cots)


def local(frames, seg, look_back, w_dw, w_qkv, w_o, cotangent):
    rows, width = frames.shape
    assert rows == STRETCH
    dp_count = lax.axis_size("dp")
    tm_count = lax.axis_size("tm")
    ring = dp_count == 4 and tm_count == 8
    part = width // dp_count

    far = shifted(frames[rows - EDGE :], "tm", 2)
    following = shifted(frames[:EDGE], "tm", -1)
    prev = shifted(frames, "tm", 1)
    same, bias = masks(look_back, seg, rows)


    if not ring:
        gathered = lax.all_gather(w_qkv, "dp", axis=1, tiled=True)
        act = conv_silu(far, prev, frames, following, same, w_dw)
        sources = [("whole", 0, (0,))]
        attn = jnp.concatenate(
            [
                attend(sources, group, [gathered], act, bias)[0]
                for group in range(width // COLS)
            ],
            1,
        )
        mixed = jnp.dot(attn, w_o, preferred_element_type=jnp.float32).astype(jnp.bfloat16)
        place = lax.axis_index("dp")
        cots = [
            lax.dynamic_slice_in_dim(cotangent, (place ^ bits) * part, part, 1)
            for bits in range(dp_count)
        ]
        cot = jnp.concatenate(
            [crossed(c, "dp", bits) if bits else c for bits, c in enumerate(cots)], 0
        )
        blocks = [attn]
        bits = 1
        while bits < dp_count:
            blocks += [crossed(block, "dp", bits) for block in blocks]
            bits *= 2
        grad = lax.dot_general(
            jnp.concatenate(blocks, 0),
            cot,
            (((0,), (0,)), ((), ())),
            preferred_element_type=jnp.float32,
        )
        return mixed, lax.psum_scatter(grad, "tm", scatter_dimension=0, tiled=True)

    mid_rows = width // 2

    sent_shape = jax.ShapeDtypeStruct((mid_rows, COLS), jnp.bfloat16)
    cot_shape = jax.ShapeDtypeStruct((rows, part), jnp.bfloat16)
    pair_shape = jax.ShapeDtypeStruct((2, mid_rows, COLS), jnp.bfloat16)
    two_shape = jax.ShapeDtypeStruct((2, rows, part), jnp.bfloat16)
    sent = sliced(first_slice, "first_slice", [pair_shape], w_qkv)[0]
    later_shapes = [sent_shape] + [cot_shape] * 2 + [two_shape]
    last, cot_own, cot_side, cot_two = sliced(
        later_slices, "later_slices", later_shapes, w_qkv, cotangent, sent
    )
    first_over = crossed(sent, "dp", 2)
    last_over = crossed(after(last, first_over), "dp", 2)
    cot_side = crossed(cot_side, "dp", 1)
    frames_here = after(frames, cot_side, last)
    act = conv_silu(far, prev, frames_here, following, same, w_dw)
    sibling = crossed(w_qkv, "dp", 1)

    def spread(block, earlier=(), relay_after=()):
        block = after(block, *earlier)
        side = crossed(block[..., : mid_rows // 2, :], "tm", 1)
        deep = crossed(block[..., mid_rows // 2 :, :], "tm", 2)
        relays = [crossed(after(b, *relay_after), "dp", 1) for b in (block, side, deep)]
        return [block, side, deep] + relays

    first_sources = [
        ("whole", 0, (0,)),
        ("whole", 1, (1,)),
        ("first", 2, (2, 3, 4)),
        ("first", 3, (5, 6, 7)),
    ]
    weights = [w_qkv, sibling] + spread(first_over, (act,))
    first_attn = attend(first_sources, 0, weights, act, bias)[0]
    far_attn = attend(first_sources, 1, weights, after(act, first_attn), bias, first_attn)[1]

    sources = first_sources + [("last", 2, (8, 9, 10)), ("last", 3, (11, 12, 13))]
    weights = weights + spread(last_over, (), (first_attn,))
    cot_over = crossed(after(cot_two, first_over), "dp", 2)
    cots = [cot_own, cot_side, cot_over, crossed(cot_over, "dp", 1)]

    def attention(turn, *earlier, ahead=()):
        return attend(sources, turn, weights, after(act, *earlier), bias, *ahead)

    far_side = crossed(far_attn, "dp", 1)
    third_attn = attention(2, far_attn, far_side)[0]
    fourth_attn, near_attn = attention(3, third_attn, ahead=(third_attn,))
    mixed = project_out([far_attn, near_attn], w_o)

    def traded(sums, *sent):
        for bits, block in enumerate(sent, 1):
            sums = sums + crossed(block, "tm", bits).astype(jnp.float32)
        return sums

    far_over = crossed(after(far_attn, cot_over), "dp", 2)
    far_relay = crossed(after(far_over, near_attn), "dp", 1)
    far_sums = traded(*grad_part([far_attn, far_side, far_over, far_relay], cots, "far"))
    far_term = crossed(far_sums.astype(jnp.bfloat16), "tm", 4)
    near_over = crossed(near_attn, "dp", 2)
    near_blocks = [near_attn, crossed(near_attn, "dp", 1), near_over, crossed(near_over, "dp", 1)]
    weight_grad = traded(*grad_part(near_blocks, cots, "near")) + far_term.astype(jnp.float32)
    return mixed, weight_grad


def solution(mesh):
    placed = (
        P(("dp", "tm"), None),
        P("dp", None),
        P("dp", None),
        P(),
        P(None, "dp"),
        P(),
        P(("dp", "tm"), None),
    )
    return jax.shard_map(
        local,
        mesh=mesh,
        in_specs=placed,
        out_specs=(P(("dp", "tm"), None), P("tm", "dp")),
        check_vma=False,
    )
```

```python
import math

import jax
import jax.numpy as jnp
from jax import lax
from jax.experimental import pallas as pl
from jax.experimental.pallas import tpu as pltpu
from jax.sharding import PartitionSpec as P

KER = 5
HDIM = 96
STRETCH = 256
GROUP = 4
COLS = GROUP * HDIM
EDGE = 16
MIB = 1 << 20
LITTLE = pl.CostEstimate(flops=10**6, bytes_accessed=10**4, transcendentals=0)

ORDERS = (
    ((0, 1, 2), (1, 2, 0), (2, 0, 1), (0, 1, 2)),
    ((2, 0, 1), (0, 1, 2), (0, 1, 2), (1, 2, 0)),
)
SENT_SLOT = [
    sum(ORDERS[f][d][r] << 2 * (4 * f + d) for f in range(2) for d in range(4)) for r in range(3)
]
SENT_ROUND = [
    sum(ORDERS[f][d].index(s) << 2 * (4 * f + d) for f in range(2) for d in range(4))
    for s in range(3)
]


def in_hbm(block):
    return pltpu.with_memory_space_constraint(block, pltpu.HBM)


def shifted(block, axis, step):
    count = lax.axis_size(axis)
    route = [(i, i + step) for i in range(count) if 0 <= i + step < count]
    return lax.ppermute(block, axis, route)


def crossed(block, axis, bits):
    count = lax.axis_size(axis)
    return lax.ppermute(block, axis, [(i, i ^ bits) for i in range(count)])


def after(block, *earlier):
    return lax.optimization_barrier((block, *earlier))[0]


def picked(packed, first, owner):
    return (packed >> (2 * (4 * first + owner))) & 3


def place_bits():
    at, place = lax.axis_index("tm"), lax.axis_index("dp")
    return at, place, 1 - at // 4, (at ^ (at >> 1)) & 1


def masks_kernel(look_ref, seg_ref, same_ref, bias_ref, segs):
    rows = bias_ref.shape[0]
    at = lax.axis_index("tm")
    half = KER // 2
    segs[...] = jnp.full(segs.shape, -1.0, jnp.float32)
    segs[:, rows + 128 : rows + 128 + seg_ref.shape[1]] = seg_ref[...].astype(jnp.float32)
    window = segs[:, pl.ds(pl.multiple_of(at * rows, 128), 2 * rows + 256)]
    mid = window[:, 128 : 128 + 2 * rows]
    lines = jnp.broadcast_to(mid, (128, 2 * rows))
    line = lax.broadcasted_iota(jnp.int32, (128, 2 * rows), 0)
    for o in range(KER):
        start = 128 + o - half
        equal = (window[:, start : start + 2 * rows] == mid).astype(jnp.float32)
        lines = jnp.where(line == o, jnp.broadcast_to(equal, lines.shape), lines)
    columns = lines.T
    same_ref[...] = columns
    col = lax.broadcasted_iota(jnp.int32, (rows, 2 * rows), 1)
    kept = (columns[rows:, KER : KER + 1] == mid) & ((col >= rows) | (look_ref[0, at] == 1))
    bias_ref[...] = jnp.where(kept, 0.0, -1e30)


def masks(look_back, seg, rows):
    vmem = pl.BlockSpec(memory_space=pltpu.VMEM)
    return pl.pallas_call(
        masks_kernel,
        out_shape=(
            jax.ShapeDtypeStruct((2 * rows, 128), jnp.float32),
            jax.ShapeDtypeStruct((rows, 2 * rows), jnp.float32),
        ),
        in_specs=[pl.BlockSpec(memory_space=pltpu.SMEM), vmem],
        out_specs=(vmem, vmem),
        scratch_shapes=[pltpu.VMEM((1, seg.shape[1] + 2 * rows + 256), jnp.float32)],
        compiler_params=pltpu.CompilerParams(vmem_limit_bytes=8 * MIB),
        cost_estimate=LITTLE,
        name="masks",
    )(look_back, seg)


def conv_kernel(far_ref, prev_ref, own_ref, next_ref, same_ref, taps_ref, act_ref, wide):
    rows = own_ref.shape[0]
    width = own_ref.shape[1]
    wide[0:EDGE] = far_ref[...].astype(jnp.float32)
    wide[EDGE : EDGE + rows] = prev_ref[...].astype(jnp.float32)
    wide[EDGE + rows : EDGE + 2 * rows] = own_ref[...].astype(jnp.float32)
    wide[EDGE + 2 * rows : 2 * EDGE + 2 * rows] = next_ref[...].astype(jnp.float32)
    part = 64
    half = KER // 2

    for start in range(0, 2 * rows, part):
        same = [
            jnp.broadcast_to(same_ref[start : start + part, o : o + 1], (part, 128))
            for o in range(KER)
        ]
        for col in range(0, width, 128):
            total = None
            for o in range(KER):
                first = EDGE + start + o - half
                term = (
                    taps_ref[o : o + 1, col : col + 128]
                    * wide[first : first + part, col : col + 128]
                )
                if o != half:
                    term = term * same[o]
                total = term if total is None else total + term
            total = 0.5 * total
            act_ref[start : start + part, col : col + 128] = (
                total + total * jnp.tanh(total)
            ).astype(jnp.bfloat16)


def conv_silu(far, prev, own, following, same, taps):
    rows, width = own.shape
    return pl.pallas_call(
        conv_kernel,
        out_shape=jax.ShapeDtypeStruct((2 * rows, width), jnp.bfloat16),
        scratch_shapes=[pltpu.VMEM((2 * EDGE + 2 * rows, width), jnp.float32)],
        compiler_params=pltpu.CompilerParams(vmem_limit_bytes=16 * MIB),
        cost_estimate=LITTLE,
        name="conv_silu",
    )(far, prev, own, following, same, taps)


def copies(pairs, sems):
    moves = [pltpu.make_async_copy(a, b, sems.at[i]) for i, (a, b) in enumerate(pairs)]
    for move in moves:
        move.start()
    for move in moves:
        move.wait()


def block_of(w_ref, turn):
    place, first, flip = place_bits()[1:]
    rows = w_ref.shape[0] // 2
    slot = picked(SENT_SLOT[turn], first, place)
    return w_ref.at[
        pl.ds(pl.multiple_of(flip * rows, rows), rows),
        pl.ds(pl.multiple_of(slot * COLS, 128), COLS),
    ]


def first_slice(w_ref, out_ref, sems):
    copies([(block_of(w_ref, turn), out_ref.at[turn]) for turn in range(2)], sems)


def later_slices(w_ref, cot_ref, _, *refs):
    place = lax.axis_index("dp")
    last, cot_own, cot_side, cot_two, sems = refs
    cots = (cot_own, cot_side, cot_two.at[0], cot_two.at[1])
    part = cot_ref.shape[1] // 4
    pairs = [(block_of(w_ref, 2), last)]
    for bits, ref in enumerate(cots):
        cols = pl.ds(pl.multiple_of((place ^ bits) * part, 128), part)
        pairs.append((cot_ref.at[:, cols], ref))
    copies(pairs, sems)


def sliced(kernel, name, out_shape, *blocks):
    anywhere = pl.BlockSpec(memory_space=pl.ANY)
    return pl.pallas_call(
        kernel,
        out_shape=out_shape,
        in_specs=[anywhere] * len(blocks),
        out_specs=[anywhere] * len(out_shape),
        scratch_shapes=[pltpu.SemaphoreType.DMA((8,))],
        compiler_params=pltpu.CompilerParams(vmem_limit_bytes=MIB),
        cost_estimate=LITTLE,
        name=name,
    )(*[in_hbm(block) for block in blocks[:2]], *blocks[2:])


def heads_kernel(sources, turn, act_ref, bias_ref, *refs):
    weight_refs, (out_ref, held, sems) = refs[:-3], refs[-3:]
    rows = out_ref.shape[0]
    width = act_ref.shape[1]
    half = width // 2
    scale = math.log2(math.e) / math.sqrt(HDIM)
    place, first, flip = place_bits()[1:]
    ring = len(sources) > 1
    if ring:
        pair = first ^ turn
    else:
        pair, flip = turn, 0
    low_half = pl.ds(pl.multiple_of(flip * half, half), half)
    high_half = pl.ds(pl.multiple_of((1 - flip) * half, half), half)

    def fetch(at):
        block = 4 * (at % 3) + 2 * pair + at // 3
        sem = sems.at[at]
        target = held.at[at]
        if ring:
            owner = (block * 11) >> 5
            slot = block - 3 * owner
            distance = owner ^ place
            code = jnp.where(
                slot == 0, SENT_ROUND[0], jnp.where(slot == 1, SENT_ROUND[1], SENT_ROUND[2])
            )
            sent_in = picked(code, first, owner)
        else:
            slot, distance = block, 0
        for form, which, refs_here in sources:
            wanted = distance == which
            if form == "first":
                wanted = wanted & (sent_in < 2)
            elif form == "last":
                wanted = wanted & (sent_in == 2)

            @pl.when(wanted)
            def _():
                if form == "whole":
                    ref = weight_refs[refs_here[0]]
                    cols = pl.ds(pl.multiple_of(slot * COLS, 128), COLS)
                    pltpu.make_async_copy(ref.at[low_half, cols], target.at[0:half], sem).start()
                    pltpu.make_async_copy(
                        ref.at[high_half, cols], target.at[half:width], sem
                    ).start()
                else:
                    start = 0
                    for index in refs_here:
                        ref = weight_refs[index]
                        if form == "first":
                            ref = ref.at[jnp.minimum(sent_in, 1)]
                        stop = start + ref.shape[0]
                        pltpu.make_async_copy(ref, target.at[start:stop], sem).start()
                        start = stop

    def wait(at):
        pltpu.make_async_copy(held.at[at], held.at[at], sems.at[at]).wait()

    def project(at, first_row):
        total = jnp.dot(
            act_ref[first_row:, low_half], held[at, 0:half], preferred_element_type=jnp.float32
        ) + jnp.dot(
            act_ref[first_row:, high_half], held[at, half:width], preferred_element_type=jnp.float32
        )
        return total.astype(jnp.bfloat16)

    def attend_group(group, queries, keys, values):
        pieces = [None] * (COLS // 128)
        for head in range(GROUP):
            low, high = head * HDIM, (head + 1) * HDIM
            first_tile, last_tile = low // 128, -(-high // 128)
            window = slice(first_tile * 128, last_tile * 128)
            base = first_tile * 128
            lane = lax.broadcasted_iota(jnp.int32, (rows, last_tile * 128 - base), 1) + base
            mine = (lane >= low) & (lane < high)
            one = jnp.where(mine, queries[:, window], jnp.zeros((), jnp.bfloat16))
            scores = lax.dot_general(
                one, keys[:, window], (((1,), (1,)), ((), ())), preferred_element_type=jnp.float32
            )
            scores = scores * scale + bias_ref[...]
            raw = jnp.exp2(scores - jnp.max(scores, axis=1, keepdims=True)).astype(jnp.bfloat16)
            spare = high if high < last_tile * 128 else low - 1
            value = values[:, window]
            at = lax.broadcasted_iota(jnp.int32, value.shape, 1) + base
            value = jnp.where(at == spare, jnp.ones((), jnp.bfloat16), value)
            mixed = jnp.dot(raw, value, preferred_element_type=jnp.float32)
            mixed = mixed * (1.0 / mixed[:, spare - base : spare - base + 1])
            for tile in range(first_tile, last_tile):
                here = slice(tile * 128 - base, (tile + 1) * 128 - base)
                if pieces[tile] is None:
                    pieces[tile] = mixed[:, here]
                else:
                    pieces[tile] = jnp.where(mine[:, here], mixed[:, here], pieces[tile])
        for tile, piece in enumerate(pieces):
            start = group * COLS + tile * 128
            out_ref[:, start : start + 128] = piece.astype(jnp.bfloat16)

    for at in range(6):
        fetch(at)
    ready = []
    for at in range(3):
        wait(at)
        ready.append(project(at, rows if at == 0 else 0))
    for at in range(3, 6):
        wait(at)
    attend_group(0, *ready)
    attend_group(1, *(project(at, rows if at == 3 else 0) for at in range(3, 6)))


def attend(sources, turn, weights, act, bias):
    rows, width = act.shape[0] // 2, act.shape[1]
    vmem = pl.BlockSpec(memory_space=pltpu.VMEM)
    anywhere = pl.BlockSpec(memory_space=pl.ANY)

    def kernel(*refs):
        heads_kernel(sources, turn, *refs)

    return pl.pallas_call(
        kernel,
        out_shape=jax.ShapeDtypeStruct((rows, 2 * COLS), jnp.bfloat16),
        in_specs=[vmem, vmem] + [anywhere] * len(weights),
        out_specs=vmem,
        scratch_shapes=[
            pltpu.VMEM((6, width, COLS), jnp.bfloat16),
            pltpu.SemaphoreType.DMA((6,)),
        ],
        compiler_params=pltpu.CompilerParams(vmem_limit_bytes=20 * MIB),
        cost_estimate=LITTLE,
        name=f"attention_{turn}",
    )(act, bias, in_hbm(weights[0]), *weights[1:])


def mixed_kernel(far_ref, near_ref, w_ref, out_ref):
    depth = far_ref.shape[1]
    first = place_bits()[2]
    far_rows, near_rows = (
        pl.ds(pl.multiple_of(pair * depth, depth), depth) for pair in (first, 1 - first)
    )
    total = jnp.dot(
        far_ref[...], w_ref[far_rows], preferred_element_type=jnp.float32
    ) + jnp.dot(near_ref[...], w_ref[near_rows], preferred_element_type=jnp.float32)
    out_ref[...] = total.astype(jnp.bfloat16)


def project_out(attns, w_o):
    rows, width = attns[0].shape[0], w_o.shape[1]
    cols = 512
    return pl.pallas_call(
        mixed_kernel,
        grid=(width // cols,),
        out_shape=jax.ShapeDtypeStruct((rows, width), jnp.bfloat16),
        in_specs=[pl.BlockSpec(attn.shape, lambda i: (0, 0)) for attn in attns]
        + [pl.BlockSpec((width, cols), lambda i: (0, i))],
        out_specs=pl.BlockSpec((rows, cols), lambda i: (0, i)),
        compiler_params=pltpu.CompilerParams(
            dimension_semantics=("arbitrary",), vmem_limit_bytes=16 * MIB
        ),
        cost_estimate=LITTLE,
        name="mixed",
    )(*attns, in_hbm(w_o))


def product(attn, cot):
    return lax.dot_general(attn, cot, (((0,), (0,)), ((), ())), preferred_element_type=jnp.float32)


def grad_kernel(*refs):
    *attn_refs, cot_0, cot_1, cot_2, cot_3, keep_ref, send_1, send_2, send_3, total = refs
    size = keep_ref.shape[0]
    low = lax.axis_index("tm") & 3
    cots = (cot_0[...], cot_1[...], cot_2[0], cot_3[1])
    total[...] = sum(product(ref[...], cot) for ref, cot in zip(attn_refs, cots))
    keep_ref[...] = total[pl.ds(pl.multiple_of(low * size, size), size)]
    for bits, ref in enumerate((send_1, send_2, send_3), 1):
        ref[...] = total[pl.ds(pl.multiple_of((low ^ bits) * size, size), size)].astype(
            jnp.bfloat16
        )


def grad_part(attns, cots, name):
    cols = cots[0].shape[1]
    size = COLS // 2
    return pl.pallas_call(
        grad_kernel,
        out_shape=[jax.ShapeDtypeStruct((size, cols), jnp.float32)]
        + [jax.ShapeDtypeStruct((size, cols), jnp.bfloat16)] * 3,
        scratch_shapes=[pltpu.VMEM((2 * COLS, cols), jnp.float32)],
        compiler_params=pltpu.CompilerParams(vmem_limit_bytes=16 * MIB),
        cost_estimate=LITTLE,
        name=name,
    )(*attns, *cots)


def local(frames, seg, look_back, w_dw, w_qkv, w_o, cotangent):
    rows, width = frames.shape
    assert rows == STRETCH
    dp_count = lax.axis_size("dp")
    tm_count = lax.axis_size("tm")
    ring = dp_count == 4 and tm_count == 8
    part = width // dp_count

    far = shifted(frames[rows - EDGE :], "tm", 2)
    following = shifted(frames[:EDGE], "tm", -1)
    prev = shifted(frames, "tm", 1)
    same, bias = masks(look_back, seg, rows)


    if not ring:
        gathered = lax.all_gather(w_qkv, "dp", axis=1, tiled=True)
        act = conv_silu(far, prev, frames, following, same, w_dw)
        sources = [("whole", 0, (0,))]
        attn = jnp.concatenate(
            [
                attend(sources, pair, [gathered], act, bias)
                for pair in range(width // COLS // 2)
            ],
            1,
        )
        mixed = jnp.dot(attn, w_o, preferred_element_type=jnp.float32).astype(jnp.bfloat16)
        place = lax.axis_index("dp")
        cots = [
            lax.dynamic_slice_in_dim(cotangent, (place ^ bits) * part, part, 1)
            for bits in range(dp_count)
        ]
        cot = jnp.concatenate(
            [crossed(c, "dp", bits) if bits else c for bits, c in enumerate(cots)], 0
        )
        blocks = [attn]
        bits = 1
        while bits < dp_count:
            blocks += [crossed(block, "dp", bits) for block in blocks]
            bits *= 2
        grad = lax.dot_general(
            jnp.concatenate(blocks, 0),
            cot,
            (((0,), (0,)), ((), ())),
            preferred_element_type=jnp.float32,
        )
        return mixed, lax.psum_scatter(grad, "tm", scatter_dimension=0, tiled=True)

    mid_rows = width // 2

    sent_shape = jax.ShapeDtypeStruct((mid_rows, COLS), jnp.bfloat16)
    cot_shape = jax.ShapeDtypeStruct((rows, part), jnp.bfloat16)
    pair_shape = jax.ShapeDtypeStruct((2, mid_rows, COLS), jnp.bfloat16)
    two_shape = jax.ShapeDtypeStruct((2, rows, part), jnp.bfloat16)
    sent = sliced(first_slice, "first_slice", [pair_shape], w_qkv)[0]
    later_shapes = [sent_shape] + [cot_shape] * 2 + [two_shape]
    last, cot_own, cot_side, cot_two = sliced(
        later_slices, "later_slices", later_shapes, w_qkv, cotangent, sent
    )
    first_over = crossed(sent, "dp", 2)
    last_over = crossed(after(last, first_over), "dp", 2)
    cot_side = crossed(cot_side, "dp", 1)
    frames_here = after(frames, cot_side, last)
    act = conv_silu(far, prev, frames_here, following, same, w_dw)
    sibling = crossed(w_qkv, "dp", 1)

    def spread(block, earlier=(), relay_after=()):
        block = after(block, *earlier)
        side = crossed(block[..., : mid_rows // 2, :], "tm", 1)
        deep = crossed(block[..., mid_rows // 2 :, :], "tm", 2)
        relays = [crossed(block, "dp", 1)]
        relays += [crossed(after(b, *relay_after), "dp", 1) for b in (side, deep)]
        return [block, side, deep] + relays

    first_sources = [
        ("whole", 0, (0,)),
        ("whole", 1, (1,)),
        ("first", 2, (2, 3, 4)),
        ("first", 3, (5, 6, 7)),
    ]
    weights = [w_qkv, sibling] + spread(first_over, (act,))
    far_attn = attend(first_sources, 0, weights, act, bias)
    far_side = crossed(far_attn, "dp", 1)

    sources = first_sources + [("last", 2, (8, 9, 10)), ("last", 3, (11, 12, 13))]
    weights = weights + spread(last_over, (), (far_attn,))
    cot_over = crossed(after(cot_two, last_over), "dp", 2)
    near_attn = attend(sources, 1, weights, after(act, far_attn), bias)
    cots = [cot_own, cot_side, cot_over, crossed(after(cot_over, near_attn), "dp", 1)]
    mixed = project_out([far_attn, near_attn], w_o)

    def traded(sums, *sent):
        for bits in (3, 2, 1):
            sums = sums + crossed(sent[bits - 1], "tm", bits).astype(jnp.float32)
        return sums

    far_over = crossed(after(far_attn, cot_over), "dp", 2)
    far_relay = crossed(after(far_over, near_attn), "dp", 1)
    far_sums = traded(*grad_part([far_attn, far_side, far_over, far_relay], cots, "far"))
    far_term = crossed(far_sums.astype(jnp.bfloat16), "tm", 4)
    near_over = crossed(near_attn, "dp", 2)
    near_blocks = [near_attn, crossed(near_attn, "dp", 1), near_over, crossed(near_over, "dp", 1)]
    weight_grad = traded(*grad_part(near_blocks, cots, "near")) + far_term.astype(jnp.float32)
    return mixed, weight_grad


def solution(mesh):
    placed = (
        P(("dp", "tm"), None),
        P("dp", None),
        P("dp", None),
        P(),
        P(None, "dp"),
        P(),
        P(("dp", "tm"), None),
    )
    return jax.shard_map(
        local,
        mesh=mesh,
        in_specs=placed,
        out_specs=(P(("dp", "tm"), None), P("tm", "dp")),
        check_vma=False,
    )
```

```python
import math

import jax
import jax.numpy as jnp
from jax import lax
from jax.experimental import pallas as pl
from jax.experimental.pallas import tpu as pltpu
from jax.sharding import PartitionSpec as P

KER = 5
HDIM = 96
STRETCH = 256
GROUP = 4
COLS = GROUP * HDIM
EDGE = 16
MIB = 1 << 20
LITTLE = pl.CostEstimate(flops=10**6, bytes_accessed=10**4, transcendentals=0)

ORDERS = (
    ((0, 1, 2), (1, 2, 0), (2, 0, 1), (0, 1, 2)),
    ((2, 0, 1), (0, 1, 2), (0, 1, 2), (1, 2, 0)),
)
SENT_SLOT = [
    sum(ORDERS[f][d][r] << 2 * (4 * f + d) for f in range(2) for d in range(4)) for r in range(3)
]
SENT_ROUND = [
    sum(ORDERS[f][d].index(s) << 2 * (4 * f + d) for f in range(2) for d in range(4))
    for s in range(3)
]


def in_hbm(block):
    return pltpu.with_memory_space_constraint(block, pltpu.HBM)


def shifted(block, axis, step):
    count = lax.axis_size(axis)
    route = [(i, i + step) for i in range(count) if 0 <= i + step < count]
    return lax.ppermute(block, axis, route)


def crossed(block, axis, bits):
    count = lax.axis_size(axis)
    return lax.ppermute(block, axis, [(i, i ^ bits) for i in range(count)])


def after(block, *earlier):
    return lax.optimization_barrier((block, *earlier))[0]


def picked(packed, first, owner):
    return (packed >> (2 * (4 * first + owner))) & 3


def place_bits():
    at, place = lax.axis_index("tm"), lax.axis_index("dp")
    return at, place, 1 - at // 4, (at ^ (at >> 1)) & 1


def masks_kernel(look_ref, seg_ref, same_ref, bias_ref, segs):
    rows = bias_ref.shape[0]
    at = lax.axis_index("tm")
    half = KER // 2
    segs[...] = jnp.full(segs.shape, -1.0, jnp.float32)
    segs[:, rows + 128 : rows + 128 + seg_ref.shape[1]] = seg_ref[...].astype(jnp.float32)
    window = segs[:, pl.ds(pl.multiple_of(at * rows, 128), 2 * rows + 256)]
    mid = window[:, 128 : 128 + 2 * rows]
    lines = jnp.broadcast_to(mid, (128, 2 * rows))
    line = lax.broadcasted_iota(jnp.int32, (128, 2 * rows), 0)
    for o in range(KER):
        start = 128 + o - half
        equal = (window[:, start : start + 2 * rows] == mid).astype(jnp.float32)
        lines = jnp.where(line == o, jnp.broadcast_to(equal, lines.shape), lines)
    columns = lines.T
    same_ref[...] = columns
    col = lax.broadcasted_iota(jnp.int32, (rows, 2 * rows), 1)
    kept = (columns[rows:, KER : KER + 1] == mid) & ((col >= rows) | (look_ref[0, at] == 1))
    bias_ref[...] = jnp.where(kept, 0.0, -1e30)


def masks(look_back, seg, rows):
    vmem = pl.BlockSpec(memory_space=pltpu.VMEM)
    return pl.pallas_call(
        masks_kernel,
        out_shape=(
            jax.ShapeDtypeStruct((2 * rows, 128), jnp.float32),
            jax.ShapeDtypeStruct((rows, 2 * rows), jnp.float32),
        ),
        in_specs=[pl.BlockSpec(memory_space=pltpu.SMEM), vmem],
        out_specs=(vmem, vmem),
        scratch_shapes=[pltpu.VMEM((1, seg.shape[1] + 2 * rows + 256), jnp.float32)],
        compiler_params=pltpu.CompilerParams(vmem_limit_bytes=8 * MIB),
        cost_estimate=LITTLE,
        name="masks",
    )(look_back, seg)


def conv_kernel(far_ref, prev_ref, own_ref, next_ref, same_ref, taps_ref, act_ref, wide):
    rows = own_ref.shape[0]
    width = own_ref.shape[1]
    wide[0:EDGE] = far_ref[...].astype(jnp.float32)
    wide[EDGE : EDGE + rows] = prev_ref[...].astype(jnp.float32)
    wide[EDGE + rows : EDGE + 2 * rows] = own_ref[...].astype(jnp.float32)
    wide[EDGE + 2 * rows : 2 * EDGE + 2 * rows] = next_ref[...].astype(jnp.float32)
    part = 64
    half = KER // 2

    for start in range(0, 2 * rows, part):
        same = [
            jnp.broadcast_to(same_ref[start : start + part, o : o + 1], (part, 128))
            for o in range(KER)
        ]
        for col in range(0, width, 128):
            total = None
            for o in range(KER):
                first = EDGE + start + o - half
                term = (
                    taps_ref[o : o + 1, col : col + 128]
                    * wide[first : first + part, col : col + 128]
                )
                if o != half:
                    term = term * same[o]
                total = term if total is None else total + term
            total = 0.5 * total
            act_ref[start : start + part, col : col + 128] = (
                total + total * jnp.tanh(total)
            ).astype(jnp.bfloat16)


def conv_silu(far, prev, own, following, same, taps):
    rows, width = own.shape
    return pl.pallas_call(
        conv_kernel,
        out_shape=jax.ShapeDtypeStruct((2 * rows, width), jnp.bfloat16),
        scratch_shapes=[pltpu.VMEM((2 * EDGE + 2 * rows, width), jnp.float32)],
        compiler_params=pltpu.CompilerParams(vmem_limit_bytes=16 * MIB),
        cost_estimate=LITTLE,
        name="conv_silu",
    )(far, prev, own, following, same, taps)


def copies(pairs, sems):
    moves = [pltpu.make_async_copy(a, b, sems.at[i]) for i, (a, b) in enumerate(pairs)]
    for move in moves:
        move.start()
    for move in moves:
        move.wait()


def block_of(w_ref, turn):
    place, first, flip = place_bits()[1:]
    rows = w_ref.shape[0] // 2
    slot = picked(SENT_SLOT[turn], first, place)
    return w_ref.at[
        pl.ds(pl.multiple_of(flip * rows, rows), rows),
        pl.ds(pl.multiple_of(slot * COLS, 128), COLS),
    ]


def first_slice(w_ref, out_ref, sems):
    copies([(block_of(w_ref, turn), out_ref.at[turn]) for turn in range(2)], sems)


def later_slices(w_ref, cot_ref, _, *refs):
    place = lax.axis_index("dp")
    last, cot_own, cot_side, cot_two, sems = refs
    cots = (cot_own, cot_side, cot_two.at[0], cot_two.at[1])
    part = cot_ref.shape[1] // 4
    pairs = [(block_of(w_ref, 2), last)]
    for bits, ref in enumerate(cots):
        cols = pl.ds(pl.multiple_of((place ^ bits) * part, 128), part)
        pairs.append((cot_ref.at[:, cols], ref))
    copies(pairs, sems)


def sliced(kernel, name, out_shape, *blocks):
    anywhere = pl.BlockSpec(memory_space=pl.ANY)
    return pl.pallas_call(
        kernel,
        out_shape=out_shape,
        in_specs=[anywhere] * len(blocks),
        out_specs=[anywhere] * len(out_shape),
        scratch_shapes=[pltpu.SemaphoreType.DMA((8,))],
        compiler_params=pltpu.CompilerParams(vmem_limit_bytes=MIB),
        cost_estimate=LITTLE,
        name=name,
    )(*[in_hbm(block) for block in blocks[:2]], *blocks[2:])


def heads_kernel(sources, turn, act_ref, bias_ref, *refs):
    weight_refs, (out_ref, held, sems) = refs[:-3], refs[-3:]
    rows = out_ref.shape[0]
    width = act_ref.shape[1]
    half = width // 2
    scale = math.log2(math.e) / math.sqrt(HDIM)
    place, first, flip = place_bits()[1:]
    ring = len(sources) > 1
    if ring:
        pair = first ^ turn
    else:
        pair, flip = turn, 0
    low_half = pl.ds(pl.multiple_of(flip * half, half), half)
    high_half = pl.ds(pl.multiple_of((1 - flip) * half, half), half)

    def fetch(at):
        block = 4 * (at % 3) + 2 * pair + at // 3
        sem = sems.at[at]
        target = held.at[at]
        if ring:
            owner = (block * 11) >> 5
            slot = block - 3 * owner
            distance = owner ^ place
            code = jnp.where(
                slot == 0, SENT_ROUND[0], jnp.where(slot == 1, SENT_ROUND[1], SENT_ROUND[2])
            )
            sent_in = picked(code, first, owner)
        else:
            slot, distance = block, 0
        for form, which, refs_here in sources:
            wanted = distance == which
            if form == "first":
                wanted = wanted & (sent_in < 2)
            elif form == "last":
                wanted = wanted & (sent_in == 2)

            @pl.when(wanted)
            def _():
                if form == "whole":
                    ref = weight_refs[refs_here[0]]
                    cols = pl.ds(pl.multiple_of(slot * COLS, 128), COLS)
                    pltpu.make_async_copy(ref.at[low_half, cols], target.at[0:half], sem).start()
                    pltpu.make_async_copy(
                        ref.at[high_half, cols], target.at[half:width], sem
                    ).start()
                else:
                    start = 0
                    for index in refs_here:
                        ref = weight_refs[index]
                        if form == "first":
                            ref = ref.at[jnp.minimum(sent_in, 1)]
                        stop = start + ref.shape[0]
                        pltpu.make_async_copy(ref, target.at[start:stop], sem).start()
                        start = stop

    def wait(at):
        pltpu.make_async_copy(held.at[at], held.at[at], sems.at[at]).wait()

    def project(at, first_row):
        total = jnp.dot(
            act_ref[first_row:, low_half], held[at, 0:half], preferred_element_type=jnp.float32
        ) + jnp.dot(
            act_ref[first_row:, high_half], held[at, half:width], preferred_element_type=jnp.float32
        )
        return total.astype(jnp.bfloat16)

    def attend_group(group, queries, keys, values):
        pieces = [None] * (COLS // 128)
        for head in range(GROUP):
            low, high = head * HDIM, (head + 1) * HDIM
            first_tile, last_tile = low // 128, -(-high // 128)
            window = slice(first_tile * 128, last_tile * 128)
            base = first_tile * 128
            lane = lax.broadcasted_iota(jnp.int32, (rows, last_tile * 128 - base), 1) + base
            mine = (lane >= low) & (lane < high)
            one = jnp.where(mine, queries[:, window], jnp.zeros((), jnp.bfloat16))
            scores = lax.dot_general(
                one, keys[:, window], (((1,), (1,)), ((), ())), preferred_element_type=jnp.float32
            )
            scores = scores * scale + bias_ref[...]
            raw = jnp.exp2(scores - jnp.max(scores, axis=1, keepdims=True)).astype(jnp.bfloat16)
            spare = high if high < last_tile * 128 else low - 1
            value = values[:, window]
            at = lax.broadcasted_iota(jnp.int32, value.shape, 1) + base
            value = jnp.where(at == spare, jnp.ones((), jnp.bfloat16), value)
            mixed = jnp.dot(raw, value, preferred_element_type=jnp.float32)
            mixed = mixed * (1.0 / mixed[:, spare - base : spare - base + 1])
            for tile in range(first_tile, last_tile):
                here = slice(tile * 128 - base, (tile + 1) * 128 - base)
                if pieces[tile] is None:
                    pieces[tile] = mixed[:, here]
                else:
                    pieces[tile] = jnp.where(mine[:, here], mixed[:, here], pieces[tile])
        for tile, piece in enumerate(pieces):
            start = group * COLS + tile * 128
            out_ref[:, start : start + 128] = piece.astype(jnp.bfloat16)

    for at in range(6):
        fetch(at)
    for at in range(3):
        wait(at)
    ready = [project(at, rows if at == 0 else 0) for at in range(3)]
    for at in range(3, 6):
        wait(at)
    attend_group(0, *ready)
    attend_group(1, *(project(at, rows if at == 3 else 0) for at in range(3, 6)))


def attend(sources, turn, weights, act, bias):
    rows, width = act.shape[0] // 2, act.shape[1]
    vmem = pl.BlockSpec(memory_space=pltpu.VMEM)
    anywhere = pl.BlockSpec(memory_space=pl.ANY)

    def kernel(*refs):
        heads_kernel(sources, turn, *refs)

    return pl.pallas_call(
        kernel,
        out_shape=jax.ShapeDtypeStruct((rows, 2 * COLS), jnp.bfloat16),
        in_specs=[vmem, vmem] + [anywhere] * len(weights),
        out_specs=vmem,
        scratch_shapes=[
            pltpu.VMEM((6, width, COLS), jnp.bfloat16),
            pltpu.SemaphoreType.DMA((6,)),
        ],
        compiler_params=pltpu.CompilerParams(vmem_limit_bytes=20 * MIB),
        cost_estimate=LITTLE,
        name=f"attention_{turn}",
    )(act, bias, in_hbm(weights[0]), *weights[1:])


def mixed_kernel(far_ref, near_ref, w_ref, out_ref):
    depth = far_ref.shape[1]
    first = place_bits()[2]
    far_rows, near_rows = (
        pl.ds(pl.multiple_of(pair * depth, depth), depth) for pair in (first, 1 - first)
    )
    total = jnp.dot(
        far_ref[...], w_ref[far_rows], preferred_element_type=jnp.float32
    ) + jnp.dot(near_ref[...], w_ref[near_rows], preferred_element_type=jnp.float32)
    out_ref[...] = total.astype(jnp.bfloat16)


def project_out(attns, w_o):
    rows, width = attns[0].shape[0], w_o.shape[1]
    cols = 512
    return pl.pallas_call(
        mixed_kernel,
        grid=(width // cols,),
        out_shape=jax.ShapeDtypeStruct((rows, width), jnp.bfloat16),
        in_specs=[pl.BlockSpec(attn.shape, lambda i: (0, 0)) for attn in attns]
        + [pl.BlockSpec((width, cols), lambda i: (0, i))],
        out_specs=pl.BlockSpec((rows, cols), lambda i: (0, i)),
        compiler_params=pltpu.CompilerParams(
            dimension_semantics=("arbitrary",), vmem_limit_bytes=16 * MIB
        ),
        cost_estimate=LITTLE,
        name="mixed",
    )(*attns, in_hbm(w_o))


def product(attn, cot):
    return lax.dot_general(attn, cot, (((0,), (0,)), ((), ())), preferred_element_type=jnp.float32)


def grad_kernel(*refs):
    *attn_refs, cot_0, cot_1, cot_2, cot_3, keep_ref, send_1, send_2, send_3, total = refs
    size = keep_ref.shape[0]
    low = lax.axis_index("tm") & 3
    cots = (cot_0[...], cot_1[...], cot_2[0], cot_3[1])
    total[...] = sum(product(ref[...], cot) for ref, cot in zip(attn_refs, cots))
    keep_ref[...] = total[pl.ds(pl.multiple_of(low * size, size), size)]
    for bits, ref in enumerate((send_1, send_2, send_3), 1):
        ref[...] = total[pl.ds(pl.multiple_of((low ^ bits) * size, size), size)].astype(
            jnp.bfloat16
        )


def grad_part(attns, cots, name):
    cols = cots[0].shape[1]
    size = COLS // 2
    return pl.pallas_call(
        grad_kernel,
        out_shape=[jax.ShapeDtypeStruct((size, cols), jnp.float32)]
        + [jax.ShapeDtypeStruct((size, cols), jnp.bfloat16)] * 3,
        scratch_shapes=[pltpu.VMEM((2 * COLS, cols), jnp.float32)],
        compiler_params=pltpu.CompilerParams(vmem_limit_bytes=16 * MIB),
        cost_estimate=LITTLE,
        name=name,
    )(*attns, *cots)


def local(frames, seg, look_back, w_dw, w_qkv, w_o, cotangent):
    rows, width = frames.shape
    assert rows == STRETCH
    dp_count = lax.axis_size("dp")
    tm_count = lax.axis_size("tm")
    ring = dp_count == 4 and tm_count == 8
    part = width // dp_count

    far = shifted(frames[rows - EDGE :], "tm", 2)
    following = shifted(frames[:EDGE], "tm", -1)
    prev = shifted(frames, "tm", 1)
    same, bias = masks(look_back, seg, rows)


    if not ring:
        gathered = lax.all_gather(w_qkv, "dp", axis=1, tiled=True)
        act = conv_silu(far, prev, frames, following, same, w_dw)
        sources = [("whole", 0, (0,))]
        attn = jnp.concatenate(
            [
                attend(sources, pair, [gathered], act, bias)
                for pair in range(width // COLS // 2)
            ],
            1,
        )
        mixed = jnp.dot(attn, w_o, preferred_element_type=jnp.float32).astype(jnp.bfloat16)
        place = lax.axis_index("dp")
        cots = [
            lax.dynamic_slice_in_dim(cotangent, (place ^ bits) * part, part, 1)
            for bits in range(dp_count)
        ]
        cot = jnp.concatenate(
            [crossed(c, "dp", bits) if bits else c for bits, c in enumerate(cots)], 0
        )
        blocks = [attn]
        bits = 1
        while bits < dp_count:
            blocks += [crossed(block, "dp", bits) for block in blocks]
            bits *= 2
        grad = lax.dot_general(
            jnp.concatenate(blocks, 0),
            cot,
            (((0,), (0,)), ((), ())),
            preferred_element_type=jnp.float32,
        )
        return mixed, lax.psum_scatter(grad, "tm", scatter_dimension=0, tiled=True)

    mid_rows = width // 2

    sent_shape = jax.ShapeDtypeStruct((mid_rows, COLS), jnp.bfloat16)
    cot_shape = jax.ShapeDtypeStruct((rows, part), jnp.bfloat16)
    pair_shape = jax.ShapeDtypeStruct((2, mid_rows, COLS), jnp.bfloat16)
    two_shape = jax.ShapeDtypeStruct((2, rows, part), jnp.bfloat16)
    sent = sliced(first_slice, "first_slice", [pair_shape], w_qkv)[0]
    later_shapes = [sent_shape] + [cot_shape] * 2 + [two_shape]
    last, cot_own, cot_side, cot_two = sliced(
        later_slices, "later_slices", later_shapes, w_qkv, cotangent, sent
    )
    first_over = crossed(sent, "dp", 2)
    last_over = crossed(after(last, first_over), "dp", 2)
    cot_side = crossed(cot_side, "dp", 1)
    frames_here = after(frames, cot_side, last)
    act = conv_silu(far, prev, frames_here, following, same, w_dw)
    sibling = crossed(w_qkv, "dp", 1)

    def spread(block, earlier=(), relay_after=()):
        block = after(block, *earlier)
        side = crossed(block[..., : mid_rows // 2, :], "tm", 1)
        deep = crossed(block[..., mid_rows // 2 :, :], "tm", 2)
        relays = [crossed(block, "dp", 1)]
        relays += [crossed(after(b, *relay_after), "dp", 1) for b in (side, deep)]
        return [block, side, deep] + relays

    first_sources = [
        ("whole", 0, (0,)),
        ("whole", 1, (1,)),
        ("first", 2, (2, 3, 4)),
        ("first", 3, (5, 6, 7)),
    ]
    weights = [w_qkv, sibling] + spread(first_over, (act,))
    far_attn = attend(first_sources, 0, weights, act, bias)
    far_side = crossed(far_attn, "dp", 1)

    sources = first_sources + [("last", 2, (8, 9, 10)), ("last", 3, (11, 12, 13))]
    weights = weights + spread(last_over, (), (far_attn,))
    cot_over = crossed(after(cot_two, last_over), "dp", 2)
    near_attn = attend(sources, 1, weights, after(act, far_attn), bias)
    cots = [cot_own, cot_side, cot_over, crossed(after(cot_over, near_attn), "dp", 1)]
    mixed = project_out([far_attn, near_attn], w_o)

    def traded(sums, *sent):
        for bits in (3, 2, 1):
            sums = sums + crossed(sent[bits - 1], "tm", bits).astype(jnp.float32)
        return sums

    far_over = crossed(after(far_attn, cot_over), "dp", 2)
    far_relay = crossed(after(far_over, near_attn), "dp", 1)
    far_sums = traded(*grad_part([far_attn, far_side, far_over, far_relay], cots, "far"))
    far_term = crossed(far_sums.astype(jnp.bfloat16), "tm", 4)
    near_over = crossed(near_attn, "dp", 2)
    near_blocks = [near_attn, crossed(near_attn, "dp", 1), near_over, crossed(near_over, "dp", 1)]
    weight_grad = traded(*grad_part(near_blocks, cots, "near")) + far_term.astype(jnp.float32)
    return mixed, weight_grad


def solution(mesh):
    placed = (
        P(("dp", "tm"), None),
        P("dp", None),
        P("dp", None),
        P(),
        P(None, "dp"),
        P(),
        P(("dp", "tm"), None),
    )
    return jax.shard_map(
        local,
        mesh=mesh,
        in_specs=placed,
        out_specs=(P(("dp", "tm"), None), P("tm", "dp")),
        check_vma=False,
    )
```

```python
import math

import jax
import jax.numpy as jnp
from jax import lax
from jax.experimental import pallas as pl
from jax.experimental.pallas import tpu as pltpu
from jax.sharding import PartitionSpec as P

KER = 5
HDIM = 96
STRETCH = 256
GROUP = 4
COLS = GROUP * HDIM
EDGE = 16
MIB = 1 << 20
LITTLE = pl.CostEstimate(flops=10**6, bytes_accessed=10**4, transcendentals=0)

ORDERS = (
    ((0, 1, 2), (1, 2, 0), (2, 0, 1), (0, 1, 2)),
    ((2, 0, 1), (0, 1, 2), (0, 1, 2), (1, 2, 0)),
)
SENT_SLOT = [
    sum(ORDERS[f][d][r] << 2 * (4 * f + d) for f in range(2) for d in range(4)) for r in range(3)
]
SENT_ROUND = [
    sum(ORDERS[f][d].index(s) << 2 * (4 * f + d) for f in range(2) for d in range(4))
    for s in range(3)
]


def in_hbm(block):
    return pltpu.with_memory_space_constraint(block, pltpu.HBM)


def shifted(block, axis, step):
    count = lax.axis_size(axis)
    route = [(i, i + step) for i in range(count) if 0 <= i + step < count]
    return lax.ppermute(block, axis, route)


def crossed(block, axis, bits):
    count = lax.axis_size(axis)
    return lax.ppermute(block, axis, [(i, i ^ bits) for i in range(count)])


def after(block, *earlier):
    return lax.optimization_barrier((block, *earlier))[0]


def picked(packed, first, owner):
    return (packed >> (2 * (4 * first + owner))) & 3


def place_bits():
    at, place = lax.axis_index("tm"), lax.axis_index("dp")
    return at, place, 1 - at // 4, (at ^ (at >> 1)) & 1


def masks_kernel(look_ref, seg_ref, same_ref, bias_ref, segs):
    rows = bias_ref.shape[0]
    at = lax.axis_index("tm")
    half = KER // 2
    segs[...] = jnp.full(segs.shape, -1.0, jnp.float32)
    segs[:, rows + 128 : rows + 128 + seg_ref.shape[1]] = seg_ref[...].astype(jnp.float32)
    window = segs[:, pl.ds(pl.multiple_of(at * rows, 128), 2 * rows + 256)]
    mid = window[:, 128 : 128 + 2 * rows]
    lines = jnp.broadcast_to(mid, (128, 2 * rows))
    line = lax.broadcasted_iota(jnp.int32, (128, 2 * rows), 0)
    for o in range(KER):
        start = 128 + o - half
        equal = (window[:, start : start + 2 * rows] == mid).astype(jnp.float32)
        lines = jnp.where(line == o, jnp.broadcast_to(equal, lines.shape), lines)
    columns = lines.T
    same_ref[...] = columns
    col = lax.broadcasted_iota(jnp.int32, (rows, 2 * rows), 1)
    kept = (columns[rows:, KER : KER + 1] == mid) & ((col >= rows) | (look_ref[0, at] == 1))
    bias_ref[...] = jnp.where(kept, 0.0, -1e30)


def masks(look_back, seg, rows):
    vmem = pl.BlockSpec(memory_space=pltpu.VMEM)
    return pl.pallas_call(
        masks_kernel,
        out_shape=(
            jax.ShapeDtypeStruct((2 * rows, 128), jnp.float32),
            jax.ShapeDtypeStruct((rows, 2 * rows), jnp.float32),
        ),
        in_specs=[pl.BlockSpec(memory_space=pltpu.SMEM), vmem],
        out_specs=(vmem, vmem),
        scratch_shapes=[pltpu.VMEM((1, seg.shape[1] + 2 * rows + 256), jnp.float32)],
        compiler_params=pltpu.CompilerParams(vmem_limit_bytes=8 * MIB),
        cost_estimate=LITTLE,
        name="masks",
    )(look_back, seg)


def conv_kernel(far_ref, prev_ref, own_ref, next_ref, same_ref, taps_ref, act_ref, wide):
    rows = own_ref.shape[0]
    width = own_ref.shape[1]
    wide[0:EDGE] = far_ref[...].astype(jnp.float32)
    wide[EDGE : EDGE + rows] = prev_ref[...].astype(jnp.float32)
    wide[EDGE + rows : EDGE + 2 * rows] = own_ref[...].astype(jnp.float32)
    wide[EDGE + 2 * rows : 2 * EDGE + 2 * rows] = next_ref[...].astype(jnp.float32)
    part = 64
    half = KER // 2

    for start in range(0, 2 * rows, part):
        same = [
            jnp.broadcast_to(same_ref[start : start + part, o : o + 1], (part, 128))
            for o in range(KER)
        ]
        for col in range(0, width, 128):
            total = None
            for o in range(KER):
                first = EDGE + start + o - half
                term = (
                    taps_ref[o : o + 1, col : col + 128]
                    * wide[first : first + part, col : col + 128]
                )
                if o != half:
                    term = term * same[o]
                total = term if total is None else total + term
            total = 0.5 * total
            act_ref[start : start + part, col : col + 128] = (
                total + total * jnp.tanh(total)
            ).astype(jnp.bfloat16)


def conv_silu(far, prev, own, following, same, taps):
    rows, width = own.shape
    return pl.pallas_call(
        conv_kernel,
        out_shape=jax.ShapeDtypeStruct((2 * rows, width), jnp.bfloat16),
        scratch_shapes=[pltpu.VMEM((2 * EDGE + 2 * rows, width), jnp.float32)],
        compiler_params=pltpu.CompilerParams(vmem_limit_bytes=16 * MIB),
        cost_estimate=LITTLE,
        name="conv_silu",
    )(far, prev, own, following, same, taps)


def copies(pairs, sems):
    moves = [pltpu.make_async_copy(a, b, sems.at[i]) for i, (a, b) in enumerate(pairs)]
    for move in moves:
        move.start()
    for move in moves:
        move.wait()


def block_of(w_ref, turn):
    place, first, flip = place_bits()[1:]
    rows = w_ref.shape[0] // 2
    slot = picked(SENT_SLOT[turn], first, place)
    return w_ref.at[
        pl.ds(pl.multiple_of(flip * rows, rows), rows),
        pl.ds(pl.multiple_of(slot * COLS, 128), COLS),
    ]


def first_slice(w_ref, out_ref, sems):
    copies([(block_of(w_ref, turn), out_ref.at[turn]) for turn in range(2)], sems)


def later_slices(w_ref, cot_ref, _, *refs):
    place = lax.axis_index("dp")
    last, cot_own, cot_side, cot_two, sems = refs
    cots = (cot_own, cot_side, cot_two.at[0], cot_two.at[1])
    part = cot_ref.shape[1] // 4
    pairs = [(block_of(w_ref, 2), last)]
    for bits, ref in enumerate(cots):
        cols = pl.ds(pl.multiple_of((place ^ bits) * part, 128), part)
        pairs.append((cot_ref.at[:, cols], ref))
    copies(pairs, sems)


def sliced(kernel, name, out_shape, *blocks):
    anywhere = pl.BlockSpec(memory_space=pl.ANY)
    return pl.pallas_call(
        kernel,
        out_shape=out_shape,
        in_specs=[anywhere] * len(blocks),
        out_specs=[anywhere] * len(out_shape),
        scratch_shapes=[pltpu.SemaphoreType.DMA((8,))],
        compiler_params=pltpu.CompilerParams(vmem_limit_bytes=MIB),
        cost_estimate=LITTLE,
        name=name,
    )(*[in_hbm(block) for block in blocks[:2]], *blocks[2:])


def heads_kernel(sources, turn, act_ref, bias_ref, *refs):
    weight_refs, (out_ref, held, sems) = refs[:-3], refs[-3:]
    rows = out_ref.shape[0]
    width = act_ref.shape[1]
    half = width // 2
    scale = math.log2(math.e) / math.sqrt(HDIM)
    place, first, flip = place_bits()[1:]
    ring = len(sources) > 1
    if ring:
        pair = first ^ turn
    else:
        pair, flip = turn, 0
    low_half = pl.ds(pl.multiple_of(flip * half, half), half)
    high_half = pl.ds(pl.multiple_of((1 - flip) * half, half), half)

    def fetch(at):
        block = 4 * (at % 3) + 2 * pair + at // 3
        sem = sems.at[at]
        target = held.at[at]
        if ring:
            owner = (block * 11) >> 5
            slot = block - 3 * owner
            distance = owner ^ place
            code = jnp.where(
                slot == 0, SENT_ROUND[0], jnp.where(slot == 1, SENT_ROUND[1], SENT_ROUND[2])
            )
            sent_in = picked(code, first, owner)
        else:
            slot, distance = block, 0
        for form, which, refs_here in sources:
            wanted = distance == which
            if form == "first":
                wanted = wanted & (sent_in < 2)
            elif form == "last":
                wanted = wanted & (sent_in == 2)

            @pl.when(wanted)
            def _():
                if form == "whole":
                    ref = weight_refs[refs_here[0]]
                    cols = pl.ds(pl.multiple_of(slot * COLS, 128), COLS)
                    pltpu.make_async_copy(ref.at[low_half, cols], target.at[0:half], sem).start()
                    pltpu.make_async_copy(
                        ref.at[high_half, cols], target.at[half:width], sem
                    ).start()
                else:
                    start = 0
                    for index in refs_here:
                        ref = weight_refs[index]
                        if form == "first":
                            ref = ref.at[jnp.minimum(sent_in, 1)]
                        stop = start + ref.shape[0]
                        pltpu.make_async_copy(ref, target.at[start:stop], sem).start()
                        start = stop

    def wait(at):
        pltpu.make_async_copy(held.at[at], held.at[at], sems.at[at]).wait()

    def project(at, first_row):
        total = jnp.dot(
            act_ref[first_row:, low_half], held[at, 0:half], preferred_element_type=jnp.float32
        ) + jnp.dot(
            act_ref[first_row:, high_half], held[at, half:width], preferred_element_type=jnp.float32
        )
        return total.astype(jnp.bfloat16)

    def attend_group(group, queries, keys, values):
        pieces = [None] * (COLS // 128)
        for head in range(GROUP):
            low, high = head * HDIM, (head + 1) * HDIM
            first_tile, last_tile = low // 128, -(-high // 128)
            window = slice(first_tile * 128, last_tile * 128)
            base = first_tile * 128
            lane = lax.broadcasted_iota(jnp.int32, (rows, last_tile * 128 - base), 1) + base
            mine = (lane >= low) & (lane < high)
            one = jnp.where(mine, queries[:, window], jnp.zeros((), jnp.bfloat16))
            scores = lax.dot_general(
                one, keys[:, window], (((1,), (1,)), ((), ())), preferred_element_type=jnp.float32
            )
            scores = scores * scale + bias_ref[...]
            raw = jnp.exp2(scores - jnp.max(scores, axis=1, keepdims=True)).astype(jnp.bfloat16)
            spare = high if high < last_tile * 128 else low - 1
            value = values[:, window]
            at = lax.broadcasted_iota(jnp.int32, value.shape, 1) + base
            value = jnp.where(at == spare, jnp.ones((), jnp.bfloat16), value)
            mixed = jnp.dot(raw, value, preferred_element_type=jnp.float32)
            mixed = mixed * (1.0 / mixed[:, spare - base : spare - base + 1])
            for tile in range(first_tile, last_tile):
                here = slice(tile * 128 - base, (tile + 1) * 128 - base)
                if pieces[tile] is None:
                    pieces[tile] = mixed[:, here]
                else:
                    pieces[tile] = jnp.where(mine[:, here], mixed[:, here], pieces[tile])
        for tile, piece in enumerate(pieces):
            start = group * COLS + tile * 128
            out_ref[:, start : start + 128] = piece.astype(jnp.bfloat16)

    for at in range(6):
        fetch(at)
    for at in range(6):
        wait(at)
    attend_group(0, *(project(at, rows if at == 0 else 0) for at in range(3)))
    attend_group(1, *(project(at, rows if at == 3 else 0) for at in range(3, 6)))


def attend(sources, turn, weights, act, bias):
    rows, width = act.shape[0] // 2, act.shape[1]
    vmem = pl.BlockSpec(memory_space=pltpu.VMEM)
    anywhere = pl.BlockSpec(memory_space=pl.ANY)

    def kernel(*refs):
        heads_kernel(sources, turn, *refs)

    return pl.pallas_call(
        kernel,
        out_shape=jax.ShapeDtypeStruct((rows, 2 * COLS), jnp.bfloat16),
        in_specs=[vmem, vmem] + [anywhere] * len(weights),
        out_specs=vmem,
        scratch_shapes=[
            pltpu.VMEM((6, width, COLS), jnp.bfloat16),
            pltpu.SemaphoreType.DMA((6,)),
        ],
        compiler_params=pltpu.CompilerParams(vmem_limit_bytes=20 * MIB),
        cost_estimate=LITTLE,
        name=f"attention_{turn}",
    )(act, bias, in_hbm(weights[0]), *weights[1:])


def mixed_kernel(far_ref, near_ref, w_ref, out_ref):
    depth = far_ref.shape[1]
    first = place_bits()[2]
    far_rows, near_rows = (
        pl.ds(pl.multiple_of(pair * depth, depth), depth) for pair in (first, 1 - first)
    )
    total = jnp.dot(
        far_ref[...], w_ref[far_rows], preferred_element_type=jnp.float32
    ) + jnp.dot(near_ref[...], w_ref[near_rows], preferred_element_type=jnp.float32)
    out_ref[...] = total.astype(jnp.bfloat16)


def project_out(attns, w_o):
    rows, width = attns[0].shape[0], w_o.shape[1]
    cols = 512
    return pl.pallas_call(
        mixed_kernel,
        grid=(width // cols,),
        out_shape=jax.ShapeDtypeStruct((rows, width), jnp.bfloat16),
        in_specs=[pl.BlockSpec(attn.shape, lambda i: (0, 0)) for attn in attns]
        + [pl.BlockSpec((width, cols), lambda i: (0, i))],
        out_specs=pl.BlockSpec((rows, cols), lambda i: (0, i)),
        compiler_params=pltpu.CompilerParams(
            dimension_semantics=("arbitrary",), vmem_limit_bytes=16 * MIB
        ),
        cost_estimate=LITTLE,
        name="mixed",
    )(*attns, in_hbm(w_o))


def product(attn, cot):
    return lax.dot_general(attn, cot, (((0,), (0,)), ((), ())), preferred_element_type=jnp.float32)


def grad_kernel(*refs):
    *attn_refs, cot_0, cot_1, cot_2, cot_3, keep_ref, send_1, send_2, send_3, total = refs
    size = keep_ref.shape[0]
    low = lax.axis_index("tm") & 3
    cots = (cot_0[...], cot_1[...], cot_2[0], cot_3[1])
    total[...] = sum(product(ref[...], cot) for ref, cot in zip(attn_refs, cots))
    keep_ref[...] = total[pl.ds(pl.multiple_of(low * size, size), size)]
    for bits, ref in enumerate((send_1, send_2, send_3), 1):
        ref[...] = total[pl.ds(pl.multiple_of((low ^ bits) * size, size), size)].astype(
            jnp.bfloat16
        )


def grad_part(attns, cots, name):
    cols = cots[0].shape[1]
    size = COLS // 2
    return pl.pallas_call(
        grad_kernel,
        out_shape=[jax.ShapeDtypeStruct((size, cols), jnp.float32)]
        + [jax.ShapeDtypeStruct((size, cols), jnp.bfloat16)] * 3,
        scratch_shapes=[pltpu.VMEM((2 * COLS, cols), jnp.float32)],
        compiler_params=pltpu.CompilerParams(vmem_limit_bytes=16 * MIB),
        cost_estimate=LITTLE,
        name=name,
    )(*attns, *cots)


def local(frames, seg, look_back, w_dw, w_qkv, w_o, cotangent):
    rows, width = frames.shape
    assert rows == STRETCH
    dp_count = lax.axis_size("dp")
    tm_count = lax.axis_size("tm")
    ring = dp_count == 4 and tm_count == 8
    part = width // dp_count

    far = shifted(frames[rows - EDGE :], "tm", 2)
    following = shifted(frames[:EDGE], "tm", -1)
    prev = shifted(frames, "tm", 1)
    same, bias = masks(look_back, seg, rows)


    if not ring:
        gathered = lax.all_gather(w_qkv, "dp", axis=1, tiled=True)
        act = conv_silu(far, prev, frames, following, same, w_dw)
        sources = [("whole", 0, (0,))]
        attn = jnp.concatenate(
            [
                attend(sources, pair, [gathered], act, bias)
                for pair in range(width // COLS // 2)
            ],
            1,
        )
        mixed = jnp.dot(attn, w_o, preferred_element_type=jnp.float32).astype(jnp.bfloat16)
        place = lax.axis_index("dp")
        cots = [
            lax.dynamic_slice_in_dim(cotangent, (place ^ bits) * part, part, 1)
            for bits in range(dp_count)
        ]
        cot = jnp.concatenate(
            [crossed(c, "dp", bits) if bits else c for bits, c in enumerate(cots)], 0
        )
        blocks = [attn]
        bits = 1
        while bits < dp_count:
            blocks += [crossed(block, "dp", bits) for block in blocks]
            bits *= 2
        grad = lax.dot_general(
            jnp.concatenate(blocks, 0),
            cot,
            (((0,), (0,)), ((), ())),
            preferred_element_type=jnp.float32,
        )
        return mixed, lax.psum_scatter(grad, "tm", scatter_dimension=0, tiled=True)

    mid_rows = width // 2

    sent_shape = jax.ShapeDtypeStruct((mid_rows, COLS), jnp.bfloat16)
    cot_shape = jax.ShapeDtypeStruct((rows, part), jnp.bfloat16)
    pair_shape = jax.ShapeDtypeStruct((2, mid_rows, COLS), jnp.bfloat16)
    two_shape = jax.ShapeDtypeStruct((2, rows, part), jnp.bfloat16)
    sent = sliced(first_slice, "first_slice", [pair_shape], w_qkv)[0]
    later_shapes = [sent_shape] + [cot_shape] * 2 + [two_shape]
    last, cot_own, cot_side, cot_two = sliced(
        later_slices, "later_slices", later_shapes, w_qkv, cotangent, sent
    )
    first_over = crossed(sent, "dp", 2)
    last_over = crossed(after(last, first_over), "dp", 2)
    cot_side = crossed(cot_side, "dp", 1)
    frames_here = after(frames, cot_side, last)
    act = conv_silu(far, prev, frames_here, following, same, w_dw)
    sibling = crossed(w_qkv, "dp", 1)

    def spread(block, earlier=(), relay_after=()):
        block = after(block, *earlier)
        side = crossed(block[..., : mid_rows // 2, :], "tm", 1)
        deep = crossed(block[..., mid_rows // 2 :, :], "tm", 2)
        relays = [crossed(block, "dp", 1)]
        relays += [crossed(after(b, *relay_after), "dp", 1) for b in (side, deep)]
        return [block, side, deep] + relays

    first_sources = [
        ("whole", 0, (0,)),
        ("whole", 1, (1,)),
        ("first", 2, (2, 3, 4)),
        ("first", 3, (5, 6, 7)),
    ]
    weights = [w_qkv, sibling] + spread(first_over, (act,))
    far_attn = attend(first_sources, 0, weights, act, bias)
    far_side = crossed(far_attn, "dp", 1)

    sources = first_sources + [("last", 2, (8, 9, 10)), ("last", 3, (11, 12, 13))]
    weights = weights + spread(last_over, (), (far_attn,))
    cot_over = crossed(after(cot_two, last_over), "dp", 2)
    near_attn = attend(sources, 1, weights, after(act, far_attn), bias)
    cots = [cot_own, cot_side, cot_over, crossed(after(cot_over, near_attn), "dp", 1)]
    mixed = project_out([far_attn, near_attn], w_o)

    def traded(sums, *sent):
        for bits in (3, 2, 1):
            sums = sums + crossed(sent[bits - 1], "tm", bits).astype(jnp.float32)
        return sums

    far_over = crossed(after(far_attn, cot_over), "dp", 2)
    far_relay = crossed(after(far_over, near_attn), "dp", 1)
    far_sums = traded(*grad_part([far_attn, far_side, far_over, far_relay], cots, "far"))
    far_term = crossed(far_sums.astype(jnp.bfloat16), "tm", 4)
    near_over = crossed(near_attn, "dp", 2)
    near_blocks = [near_attn, crossed(near_attn, "dp", 1), near_over, crossed(near_over, "dp", 1)]
    weight_grad = traded(*grad_part(near_blocks, cots, "near")) + far_term.astype(jnp.float32)
    return mixed, weight_grad


def solution(mesh):
    placed = (
        P(("dp", "tm"), None),
        P("dp", None),
        P("dp", None),
        P(),
        P(None, "dp"),
        P(),
        P(("dp", "tm"), None),
    )
    return jax.shard_map(
        local,
        mesh=mesh,
        in_specs=placed,
        out_specs=(P(("dp", "tm"), None), P("tm", "dp")),
        check_vma=False,
    )
```
